512 devices in a mesh: engine: 32 (over y_hi, z), section: 16 (over x, y_lo, core).
Axes of the slice: x: 4, y: 4 (y_hi: 2, y_lo: 2; y = y_hi * 2 + y_lo), z: 16, core: 2. Of those that a mesh axis runs over, the one named last changes fastest.
Arguments:
- hidden: bfloat16 [32, 4, 5120], P('engine', None, 'section'), may hold values from -6 to 6
- stored_key_cache: bfloat16 [32, 16, 4, 256, 640], P('engine', 'section'), may hold values from -3 to 3
- values: bfloat16 [32, 16, 4, 256, 640], P('engine', 'section'), may hold values from -6 to 6
- q_gain: float32 [16, 128], P('section'), may hold values from 0.5 to 2
- out_gain: float32 [16, 5120], P('section'), may hold values from 1 to 4
- kv_len: int32 [32, 4], replicated, may hold values from 1 to 254, as said below
- migration: int32 [32, 3], replicated, may hold values from 0 to 31, as said below
Outputs:
- section_rows: bfloat16 [32, 16, 4, 5120], P('engine', 'section')
The draws below stay inside these ranges and needn't reach their ends.
Inputs may be any that keep to these rules, and one draw needn't show every extreme that they name: `kv_len`: every slot has at least one cached position and room for 2 new ones; the largest length, 254, occurs in every draw. `migration`: row e holds (slot, partner, partner slot). The partner of engine e is e itself (no swap) or the engine whose index differs from e in the lowest bit. Partners are mutual: if p is e's partner, e is p's partner, and p's first column equals e's third column. Engines 0 and 1 always swap, and so do the last two engines.
All inputs are finite; a program needn't handle non-finite values.
Results may differ from the reference program's by a relative error of at most 0.017.
Values may be sent and summed in bfloat16 or wider, within the bound.
A program may use at most 64 MiB of HBM per device.

```python
import math
import jax
import jax.numpy as jnp
from jax import lax

HEAD_WIDTH = 128
KEY_HEADS = 5
D = 5120
SLOT_TOTAL = 4
POSITION_LIMIT = 256
STEPS = 2
ENGINE_COUNT = 32
SECTION_COUNT = 16


def draw_kv_len(key, part):
    key = jax.random.fold_in(key, 11)
    key_lengths, key_marked = jax.random.split(key)
    longest = POSITION_LIMIT - STEPS
    lengths = jax.random.randint(key_lengths, (ENGINE_COUNT * SLOT_TOTAL,), 1, longest + 1)
    marked = jax.random.randint(key_marked, (), 0, ENGINE_COUNT * SLOT_TOTAL)
    return lengths.at[marked].set(longest).reshape(ENGINE_COUNT, SLOT_TOTAL).astype(jnp.int32)


def draw_migration(key, part):
    key = jax.random.fold_in(key, 23)
    key_pairs, key_slots = jax.random.split(key)
    engine_ids = jnp.arange(ENGINE_COUNT, dtype=jnp.int32)
    lower = engine_ids - engine_ids % 2
    higher = lower + 1
    other = jnp.where(engine_ids == lower, higher, lower)
    chance = jax.random.randint(key_pairs, (ENGINE_COUNT,), 0, 4)
    active = (chance[lower] != 0) | (lower == 0) | (lower == ENGINE_COUNT - 2)
    partner = jnp.where(active, other, engine_ids)
    slots_out = jax.random.randint(key_slots, (ENGINE_COUNT,), 0, SLOT_TOTAL)
    return jnp.stack([slots_out, partner, slots_out[partner]], axis=1).astype(jnp.int32)


def steps_of(own_key, dims, shards, low, high):
    def one(dim, shards_of):
        heights = jax.random.uniform(jax.random.fold_in(jax.random.fold_in(own_key, 6), dim), (shards_of,), jnp.float32, low / len(shards), high / len(shards))
        return jnp.repeat(jnp.exp(heights), dims[dim] // shards_of).reshape((-1,) + (1,) * (len(dims) - dim - 1))

    gain = one(*shards[0])
    for cut in shards[1:]:
        gain = gain * one(*cut)
    return gain


def scatter_about(rng, extent, scale, bound, cuts=(), kind=jnp.bfloat16):
    values = jax.random.normal(rng, extent, jnp.float32) * scale
    if len(cuts) > 0:
        values = steps_of(rng, extent, cuts, -0.22, 0.18) * values
    return jnp.clip(values, min=-bound, max=bound).astype(kind)


def setup_inputs(seed: int = 0) -> dict:
    key_list = jax.random.split(jax.random.key(seed), 8)
    hidden = scatter_about(key_list[0], (ENGINE_COUNT, SLOT_TOTAL, D), 1.0, 6.0, ((0, 32), (2, 16)))
    stored_key_cache = scatter_about(key_list[1], (ENGINE_COUNT, SECTION_COUNT, SLOT_TOTAL, POSITION_LIMIT, KEY_HEADS * HEAD_WIDTH), 1.0, 3.0, ((0, 32), (1, 16)))
    values = scatter_about(key_list[2], (ENGINE_COUNT, SECTION_COUNT, SLOT_TOTAL, POSITION_LIMIT, KEY_HEADS * HEAD_WIDTH), 1.0, 6.0, ((0, 32), (1, 16)))
    q_gain = jnp.clip(jnp.exp(math.log(2.0) - 1.3862944 * jax.random.uniform(key_list[3], (SECTION_COUNT, HEAD_WIDTH), jnp.float32) ** steps_of(key_list[3], (SECTION_COUNT, HEAD_WIDTH), ((0, 16),), -0.2, 0.2)), 0.5, 2.0)
    out_gain = jnp.clip(jnp.exp(math.log(4.0) - 1.3862944 * jax.random.uniform(key_list[4], (SECTION_COUNT, D), jnp.float32) ** steps_of(key_list[4], (SECTION_COUNT, D), ((0, 16),), -0.2, 0.2)), 1.0, 4.0)
    kv_len = draw_kv_len(jax.random.fold_in(key_list[7], 71), 0)
    migration = draw_migration(jax.random.fold_in(key_list[7], 71), 0)
    return {"hidden": hidden, "stored_key_cache": stored_key_cache, "values": values, "q_gain": q_gain, "out_gain": out_gain, "kv_len": kv_len, "migration": migration}


epsilon = 1e-06

def attend(row_block, keys_layer, values_layer, limit, gain_query, gain_out):
    row_count = row_block.shape[0]
    model_width = row_block.shape[1]
    head_size = gain_query.shape[0]
    positions = keys_layer.shape[1]
    kv_width = keys_layer.shape[2]
    kv_heads = kv_width // head_size
    group_size = model_width // kv_width
    widened = row_block.astype(jnp.float32).reshape(row_count, kv_heads, group_size, head_size)
    queries = (widened * lax.rsqrt(lax.optimization_barrier(jnp.mean(widened * widened, axis=-1, keepdims=True)) + epsilon) * gain_query).astype(jnp.bfloat16)
    keyed = keys_layer.reshape(row_count, positions, kv_heads, head_size)
    scores = jnp.einsum('rgqd,rcgd->rgqc', queries.astype(jnp.float32), keyed.astype(jnp.float32)) * head_size ** (-0.5)
    visible = jnp.arange(positions, dtype=jnp.int32)[None, :] < limit[:, None]
    raised = jnp.where(visible[:, None, None, :], jnp.exp(scores), 0.0)
    weights = (raised / lax.optimization_barrier(jnp.sum(raised, axis=-1, keepdims=True))).astype(jnp.bfloat16)
    valued = values_layer.reshape(row_count, positions, kv_heads, head_size)
    mixture = jnp.einsum('rgqc,rcgd->rgqd', weights.astype(jnp.float32), valued.astype(jnp.float32)).reshape(row_count, model_width)
    return (row_block.astype(jnp.float32) + gain_out * mixture).astype(jnp.bfloat16)

def reference(hidden, stored_key_cache, values, q_gain, out_gain, kv_len, migration):
    slot_index = jnp.arange(SLOT_TOTAL, dtype=jnp.int32)

    def one_engine(engine_id):
        slot_out = migration[engine_id, 0]
        partner = migration[engine_id, 1]
        partner_slot = migration[engine_id, 2]
        chosen = (slot_index == slot_out) & (partner != engine_id)
        keys_now = jnp.where(chosen[None, :, None, None], stored_key_cache[partner, :, partner_slot][:, None], stored_key_cache[engine_id])
        values_now = jnp.where(chosen[None, :, None, None], values[partner, :, partner_slot][:, None], values[engine_id])
        current = jnp.where(chosen[:, None], hidden[partner, partner_slot][None, :], hidden[engine_id])
        lengths = jnp.where(chosen, kv_len[partner, partner_slot], kv_len[engine_id])
        per_section = None
        for step in range(STEPS):
            limit = lengths + step + 1

            def through(carried, layer_inputs):
                keys_layer, values_layer, gain_query, gain_out = layer_inputs
                produced = attend(carried, keys_layer, values_layer, limit, gain_query, gain_out)
                return (produced, produced)
            current, per_section = lax.scan(through, current, (keys_now, values_now, q_gain, out_gain))
        return per_section
    return lax.map(one_engine, jnp.arange(ENGINE_COUNT, dtype=jnp.int32))
```

```python
import functools

import jax
import jax.numpy as jnp
from jax import lax
from jax.experimental import pallas as pl
from jax.experimental.pallas import tpu as pltpu
from jax.sharding import PartitionSpec as P

MESH = pl.DeviceIdType.MESH
EPSILON = 1e-06
STEPS = 2
HEAD = 128
GROUP = 8
CHUNKS = 4
HIDDEN = -1e30


def kernel(
    sections,
    kv_heads,
    kv_len_in,
    migration_in,
    hidden_in,
    q_gain_in,
    out_gain_in,
    keys,
    values,
    out,
    kv_len,
    migration,
    hidden,
    q_gain,
    out_gain,
    side,
    side_all,
    query_all,
    gain,
    gain_all,
    key_all,
    value_all,
    rows,
    hop_out,
    hop_in,
    leaving,
    landed,
    table,
    fetch,
    side_send,
    side_recv,
    query_send,
    query_recv,
    gain_send,
    gain_recv,
    cache_send,
    cache_recv,
    hop_send,
    hop_recv,
    row_send,
    row_recv,
):
    slots, positions = keys.shape[0], keys.shape[1]
    chains = slots * kv_heads
    spare = chains - sections
    half = sections // 2
    me = lax.axis_index("section")
    engine = lax.axis_index("engine")
    partner = engine + 1 - 2 * lax.rem(engine, 2)
    hosts = lax.rem(me, 2) == 0
    second = sections + me // 4
    side_of = lax.rem(me // 2, 2)
    other = me + 2 - 4 * side_of

    def shared_home(e):
        return 4 * e + 2 * (me // half)

    def landing(ref, sem):
        return pltpu.make_async_copy(ref, ref, sem)

    fetches = [
        pltpu.make_async_copy(a, b, fetch.at[i])
        for i, (a, b) in enumerate(
            (
                (hidden_in, hidden),
                (q_gain_in, q_gain),
                (out_gain_in, out_gain),
                (kv_len_in, kv_len),
                (migration_in, migration),
            )
        )
    ]
    for copy in fetches:
        copy.start()

    barrier = pltpu.get_barrier_semaphore()

    def greet(d, _):
        peer = lax.rem(me + d, sections)
        pl.semaphore_signal(barrier, inc=1, device_id=(engine, peer), device_id_type=MESH)
        return 0

    lax.fori_loop(1, sections, greet, 0)
    pl.semaphore_signal(barrier, inc=1, device_id=(partner, me), device_id_type=MESH)

    for copy in fetches:
        copy.wait()

    width = hidden.shape[1]
    wide = jnp.concatenate(
        [hidden[...].astype(jnp.float32), jnp.zeros((slots, 3 * HEAD - width), jnp.float32)], axis=1
    )
    wide = jnp.concatenate([wide, jnp.zeros((8 - slots, 3 * HEAD), jnp.float32)], axis=0)
    wide = jnp.where(lax.rem(me, 2) == 1, pltpu.roll(wide, 3 * HEAD - width, 1), wide)
    for t in range(3):
        side[t * slots : (t + 1) * slots, :] = wide[:slots, t * HEAD : (t + 1) * HEAD]
    side[3 * slots :, :] = jnp.zeros((4, HEAD), jnp.float32)
    for i in range(kv_heads * GROUP):
        gain[i : i + 1, :] = out_gain[:, i * HEAD : (i + 1) * HEAD]

    pl.semaphore_wait(barrier, sections)

    def side_copy(dest):
        return pltpu.make_async_remote_copy(
            src_ref=side, dst_ref=side_all.at[me], send_sem=side_send.at[dest], recv_sem=side_recv.at[me],
            device_id=(engine, dest), device_id_type=MESH,
        )

    def query_copy(dest):
        return pltpu.make_async_remote_copy(
            src_ref=q_gain, dst_ref=query_all.at[me], send_sem=query_send.at[dest], recv_sem=query_recv.at[me],
            device_id=(engine, dest), device_id_type=MESH,
        )

    def used(source, dest):
        def within(group):
            return (source // 2 >= group * GROUP // 5) & (source // 2 <= (group * GROUP + GROUP - 1) // 5)

        shared = (lax.rem(dest, 4) == 0) & within(lax.rem(sections + dest // 4, kv_heads))
        return within(lax.rem(dest, kv_heads)) | shared

    def gain_part(c):
        return gain.at[pl.ds(pl.multiple_of(lax.rem(c, kv_heads) * GROUP, GROUP), GROUP)]

    def gain_copy(c, dest, j):
        return pltpu.make_async_remote_copy(
            src_ref=gain_part(c), dst_ref=gain_all.at[j, me], send_sem=gain_send.at[c], recv_sem=gain_recv.at[j, me],
            device_id=(engine, dest), device_id_type=MESH,
        )

    def cache_part(array, c, start, size):
        lanes = pl.ds(pl.multiple_of(lax.rem(c, kv_heads) * HEAD, HEAD), HEAD)
        return array.at[c // kv_heads, pl.ds(start, size), lanes]

    def cache_copy(i, c, dest, j, start, size):
        return pltpu.make_async_remote_copy(
            src_ref=cache_part((keys, values)[i], c, start, size),
            dst_ref=(key_all, value_all)[i].at[j, me, pl.ds(start, size)],
            send_sem=cache_send.at[c, i], recv_sem=cache_recv.at[j, me, i],
            device_id=(engine, dest), device_id_type=MESH,
        )

    def keep(c, j):
        pltpu.make_async_copy(gain_part(c), gain_all.at[j, me], gain_recv.at[j, me]).start()
        for i in range(2):
            pltpu.make_async_copy(
                cache_part((keys, values)[i], c, 0, positions), (key_all, value_all)[i].at[j, me], cache_recv.at[j, me, i]
            ).start()

    def send_side(d, _):
        dest = lax.rem(me + sections - d, sections)

        @pl.when(used(me, dest))
        def _():
            side_copy(dest).start()

        query_copy(dest).start()
        gain_copy(dest, dest, 0).start()
        return 0

    lax.fori_loop(1, sections, send_side, 0)
    pltpu.make_async_copy(side, side_all.at[me], side_recv.at[me]).start()
    pltpu.make_async_copy(q_gain, query_all.at[me], query_recv.at[me]).start()

    def send_shared(e, _):
        dest = shared_home(e)

        @pl.when(dest != me)
        def _():
            gain_copy(sections + e, dest, 1).start()
            for i in range(2):
                cache_copy(i, sections + e, dest, 1, 0, positions).start()

        return 0

    lax.fori_loop(0, spare, send_shared, 0)

    piece = positions // CHUNKS

    def send_main(pieces, low, high):
        for k in pieces:

            def send_cache(d, _):
                column = me // 4
                i = d // 4
                column = lax.rem(column + i + (i // 2) * (1 - 2 * lax.rem(i, 2)), 4)
                dest = column * 4 + lax.rem(me + d, 4)

                @pl.when(dest != me)
                def _():
                    for i in range(2):
                        cache_copy(i, dest, dest, 0, k * piece, piece).start()

                return 0

            lax.fori_loop(low, high, send_cache, 0)

    send_main((0, 1), 0, 16)
    keep(me, 0)

    @pl.when(hosts & (me // half == side_of))
    def _():
        keep(second, 1)

    def wait_side(d, _):
        @pl.when(used(d, me) | (d == me))
        def _():
            landing(side_all.at[d], side_recv.at[d]).wait()

        landing(query_all.at[d], query_recv.at[d]).wait()
        return 0

    lax.fori_loop(0, sections, wait_side, 0)

    def enter(c):
        slot, group = c // kv_heads, lax.rem(c, kv_heads)
        for h in range(GROUP):
            head = group * GROUP + h
            pair, m = head // 5, lax.rem(head, 5)
            low = side_all[2 * pair, pl.ds(jnp.minimum(m, 2) * slots + slot, 1), :]
            high = side_all[2 * pair + 1, pl.ds(jnp.maximum(m - 2, 0) * slots + slot, 1), :]
            rows[h : h + 1, :] = jnp.where(m <= 2, low, 0.0) + jnp.where(m >= 2, high, 0.0)
        return rows[...]

    ones = jnp.ones((positions, HEAD), jnp.bfloat16)
    place = lax.broadcasted_iota(jnp.int32, (1, positions), 1)

    def tick(j, layer, r, bias):
        scale = lax.rsqrt(jnp.mean(r * r, axis=-1, keepdims=True) + EPSILON) * HEAD ** (-0.5)
        query = (r * query_all[layer]).astype(jnp.bfloat16)
        scores = lax.dot_general(
            query, key_all[j, layer], (((1,), (1,)), ((), ())), preferred_element_type=jnp.float32
        )
        raised = jnp.exp(scores * scale + bias).astype(jnp.bfloat16)
        both = jnp.dot(
            raised,
            jnp.concatenate([value_all[j, layer], ones], axis=1),
            preferred_element_type=jnp.float32,
        )
        attended = both[:, :HEAD] / both[:, HEAD:]
        return (r + gain_all[j, layer] * attended).astype(jnp.bfloat16).astype(jnp.float32)

    def bias_of(c, step):
        return jnp.where(place < kv_len[c // kv_heads, engine] + step + 1, 0.0, HIDDEN)

    def first_pass(c, j, r, low, high):
        bias = bias_of(c, 0)

        def body(step, r):
            layers = [low + step * 4 + i for i in range(4)]
            for layer in layers:
                landing(gain_all.at[j, layer], gain_recv.at[j, layer]).wait()
                for i, whole in enumerate((key_all, value_all)):
                    landing(whole.at[j, layer], cache_recv.at[j, layer, i]).wait()
            for layer in layers:
                r = tick(j, layer, r, bias)
            return r

        return lax.fori_loop(0, (high - low) // 4, body, r)

    def emit(c, j, layer, r):
        leaving[j, layer] = r
        pltpu.make_async_remote_copy(
            src_ref=leaving.at[j, layer], dst_ref=landed.at[chains + c], send_sem=row_send.at[j],
            recv_sem=row_recv, device_id=(partner, layer), device_id_type=MESH,
        ).start()

        @pl.when(layer != me)
        def _():
            pltpu.make_async_remote_copy(
                src_ref=leaving.at[j, layer], dst_ref=landed.at[c], send_sem=row_send.at[j],
                recv_sem=row_recv, device_id=(engine, layer), device_id_type=MESH,
            ).start()

        @pl.when(layer == me)
        def _():
            pltpu.make_async_copy(leaving.at[j, layer], landed.at[c], row_recv).start()

    def last_pass(c, j, r, low, high):
        bias = bias_of(c, 1)

        def body(step, r):
            layers = [low + step * 2 + i for i in range(2)]
            left = []
            for layer in layers:
                r = tick(j, layer, r, bias)
                left.append(r)
            for layer, row in zip(layers, left):
                emit(c, j, layer, row)
            return r

        return lax.fori_loop(0, (high - low) // 2, body, r)

    def last_pass_two(r, s):
        bias, bias_two = bias_of(me, 1), bias_of(second, 1)

        def body(step, carry):
            r, s = carry
            layers = [step * 2 + i for i in range(2)]
            left = []
            for layer in layers:
                r = tick(0, layer, r, bias)
                s = tick(1, layer + half, s, bias_two)
                left.append((r, s))
            for layer, (row, row_two) in zip(layers, left):
                emit(me, 0, layer, row)
                emit(second, 1, layer + half, row_two)
            return r, s

        return lax.fori_loop(0, half // 2, body, (r, s))[0]

    def hop(p):
        return pltpu.make_async_remote_copy(
            src_ref=hop_out.at[p], dst_ref=hop_in.at[p], send_sem=hop_send.at[p], recv_sem=hop_recv.at[p],
            device_id=(engine, other), device_id_type=MESH,
        )

    here = hosts & (side_of == 0)
    there = hosts & (side_of == 1)

    @pl.when(here)
    def _():
        hop_out[0] = first_pass(second, 1, enter(second), 0, half)
        hop(0).start()

    send_main((2,), 0, 16)

    @pl.when(there)
    def _():
        hop(0).wait_recv()
        hop_out[0] = first_pass(second, 1, hop_in[0], half, sections)
        hop(0).start()

    send_main((3,), 0, 16)

    @pl.when(here)
    def _():
        hop(0).wait_recv()
        hop_out[1] = last_pass(second, 1, hop_in[0], 0, half)
        hop(1).start()

    rows[...] = first_pass(me, 0, enter(me), 0, sections)

    @pl.when(there)
    def _():
        hop(1).wait_recv()
        rows[...] = last_pass_two(rows[...], hop_in[1])

    @pl.when(jnp.logical_not(there))
    def _():
        rows[...] = last_pass(me, 0, rows[...], 0, half)

    last_pass(me, 0, rows[...], half, sections)

    def sent(d, _):
        dest = lax.rem(me + d, sections)
        @pl.when(used(me, dest))
        def _():
            landing(side, side_send.at[dest]).wait()

        landing(q_gain, query_send.at[dest]).wait()
        landing(gain_part(dest), gain_send.at[dest]).wait()
        for i in range(2):
            landing(key_all.at[0, 0], cache_send.at[dest, i]).wait()
        return 0

    lax.fori_loop(1, sections, sent, 0)

    def sent_shared(e, _):
        @pl.when(shared_home(e) != me)
        def _():
            c = sections + e
            landing(gain_part(c), gain_send.at[c]).wait()
            for i in range(2):
                landing(key_all.at[0, 0], cache_send.at[c, i]).wait()

        return 0

    lax.fori_loop(0, spare, sent_shared, 0)
    landing(landed, row_recv).wait()
    moving = migration[1, engine] != engine
    for slot in range(slots):
        swapped = moving & (migration[0, engine] == slot)
        base = jnp.where(swapped, chains + migration[2, engine] * kv_heads, slot * kv_heads)
        for g in range(kv_heads):
            table[slot, g * GROUP : (g + 1) * GROUP, :] = landed[base + g]
    for head in range(kv_heads * GROUP):
        out[:, head * HEAD : (head + 1) * HEAD] = table[:, head, :].astype(out.dtype)

    landing(landed.at[pl.ds(0, 2 * sections - 1)], row_send.at[0]).wait()

    @pl.when(hosts)
    def _():
        hop(0).wait_send()

    @pl.when(hosts & (side_of == 0))
    def _():
        hop(1).wait_send()

    @pl.when(hosts & (me // half == side_of))
    def _():
        landing(landed.at[pl.ds(0, sections - 1)], row_send.at[1]).wait()

    @pl.when(hosts & (me // half != side_of))
    def _():
        landing(landed.at[pl.ds(0, sections)], row_send.at[1]).wait()


def on_device(hidden, keys, values, q_gain, out_gain, kv_len, migration):
    sections = lax.axis_size("section")
    keys, values, hidden = keys[0, 0], values[0, 0], hidden[0]
    kv_len, migration = kv_len.T, migration.T
    slots, positions, kv_width = keys.shape
    kv_heads = kv_width // HEAD
    chains = slots * kv_heads
    dma = pltpu.SemaphoreType.DMA
    vmem = pl.BlockSpec(memory_space=pltpu.VMEM)
    anywhere = pl.BlockSpec(memory_space=pltpu.HBM)
    rows = pl.pallas_call(
        functools.partial(kernel, sections, kv_heads),
        out_shape=pltpu.VMEM((slots, out_gain.shape[1]), jnp.bfloat16),
        in_specs=[anywhere] * 7,
        out_specs=vmem,
        scratch_shapes=[
            pltpu.SMEM(kv_len.shape, jnp.int32),
            pltpu.SMEM(migration.shape, jnp.int32),
            pltpu.VMEM(hidden.shape, hidden.dtype),
            pltpu.VMEM(q_gain.shape, jnp.float32),
            pltpu.VMEM(out_gain.shape, jnp.float32),
            pltpu.VMEM((16, HEAD), jnp.float32),
            pltpu.VMEM((sections, 16, HEAD), jnp.float32),
            pltpu.VMEM((sections, 1, HEAD), jnp.float32),
            pltpu.VMEM((kv_heads * GROUP, HEAD), jnp.float32),
            pltpu.VMEM((2, sections, GROUP, HEAD), jnp.float32),
            pltpu.VMEM((2, sections, positions, HEAD), jnp.bfloat16),
            pltpu.VMEM((2, sections, positions, HEAD), jnp.bfloat16),
            pltpu.VMEM((GROUP, HEAD), jnp.float32),
            pltpu.VMEM((2, GROUP, HEAD), jnp.float32),
            pltpu.VMEM((2, GROUP, HEAD), jnp.float32),
            pltpu.VMEM((2, sections, GROUP, HEAD), jnp.float32),
            pltpu.VMEM((2 * chains, GROUP, HEAD), jnp.float32),
            pltpu.VMEM((slots, kv_heads * GROUP, HEAD), jnp.float32),
            dma((5,)),
            dma((sections,)),
            dma((sections,)),
            dma((sections,)),
            dma((sections,)),
            dma((chains,)),
            dma((2, sections)),
            dma((chains, 2)),
            dma((2, sections, 2)),
            dma((2,)),
            dma((2,)),
            dma((2,)),
            dma(()),
        ],
        compiler_params=pltpu.CompilerParams(
            collective_id=0, has_side_effects=True, vmem_limit_bytes=56 * 2**20
        ),
        name="chains_at_home",
    )(kv_len, migration, hidden, q_gain, out_gain, keys, values)
    return rows[None, None]


def solution(mesh):
    in_specs = (
        P("engine", None, "section"),
        P("engine", "section", None, None, None),
        P("engine", "section", None, None, None),
        P("section", None),
        P("section", None),
        P(),
        P(),
    )
    out_specs = P("engine", "section", None, None)
    return jax.shard_map(
        on_device, mesh=mesh, in_specs=in_specs, out_specs=out_specs, check_vma=False
    )
```
